512 devices in a mesh: guide: 2 (over y_lo), patch: 64 (over x, z), tensor: 4 (over y_hi, core).
Axes of the slice: x: 4, y: 4 (y_hi: 2, y_lo: 2; y = y_hi * 2 + y_lo), z: 16, core: 2. Of those that a mesh axis runs over, the one named last changes fastest.
Arguments:
- query: bfloat16 [2, 5120, 2560], P('guide', 'patch', 'tensor'), may hold values from -160 to 160
- fresh_kv: bfloat16 [2, 2, 5120, 2560], P('guide', None, 'patch', 'tensor'), may hold values from -16 to 16
- stale_kv: bfloat16 [2, 2, 5120, 2560], P('guide', None, 'patch', 'tensor'), may hold values from -32 to 32
- assign: int32 [5120], P('patch'), may hold values from 0 to 5119, each once
- timestep: int32 [1], replicated, may hold values from 0 to 49
- gate_table: float32 [50, 5120], P(None, ('guide', 'tensor')), may hold values from -6 to 6
- residual: bfloat16 [2, 5120, 5120], P(None, 'patch', ('guide', 'tensor')), may hold values from -1.796875 to 1.796875
- out_weight: bfloat16 [2560, 5120], P('tensor', 'guide'), may hold values from -0.125 to 0.125
Outputs:
- guided: bfloat16 [5120, 5120], P('patch', ('guide', 'tensor'))
The draws below stay inside these ranges and needn't reach their ends.
All inputs are finite; a program needn't handle non-finite values.
Results may differ from the reference program's by a relative error of at most 0.015.
Values may be sent and summed in bfloat16 or wider, within the bound.
No kernel may reach another device: no remote copies, remote signals or barrier semaphores. Data moves between devices by JAX's collectives and lax.ppermute only.
A program may use at most 128 MiB of HBM per device.

```python
import jax
import jax.numpy as jnp
from jax import lax

D = 5120
HD = 128
HEADS = 20
STEPS = 50
TOK_DEV = 80
TOKENS = 5120


def shared_base(key):
    query_key, stale_key = jax.random.split(key, 2)
    query_base = jax.random.normal(query_key, (2, TOKENS, HEADS * HD), jnp.float32)
    normal_part = jax.random.normal(stale_key, (2, 2, TOKENS, HEADS * HD), jnp.float32)
    stale_base = normal_part
    return (query_base, stale_base)


def draw_query(key, part):
    query_base, stale_base = shared_base(key)
    queries = query_base
    return queries.astype(jnp.bfloat16)


def draw_stale_kv(key, part):
    query_base, stale_base = shared_base(key)
    key = jax.random.fold_in(key, 11)
    offsets = jax.random.normal(key, (2, TOKENS // TOK_DEV, HEADS * HD), jnp.float32)
    offsets = jnp.repeat(offsets, TOK_DEV, axis=1)
    stale = stale_base.at[:, 1].set(stale_base[:, 1] + 4.0 * offsets)
    return stale.astype(jnp.bfloat16)


def draw_fresh_kv(key, part):
    query_base, stale_base = shared_base(key)
    key = jax.random.fold_in(key, 5)
    key_key, value_key = jax.random.split(key)
    key_rows = 0.8 * jax.random.normal(key_key, (2, TOKENS, HEADS * HD), jnp.float32) + 0.6 * query_base
    value_rows = jax.random.normal(value_key, (2, TOKENS, HEADS * HD), jnp.float32)
    return jnp.stack([key_rows, value_rows], axis=1).astype(jnp.bfloat16)


def shard_levels(key, extent, shards, low, largest):
    gain, own = 1.0, jax.random.fold_in(key, 6)
    for dim, blocks in shards:
        draws = jnp.exp(jax.random.uniform(jax.random.fold_in(own, dim), (blocks,), jnp.float32, low / len(shards), largest / len(shards)))
        gain = gain * jnp.repeat(draws, extent[dim] // blocks).reshape([-1 if axis == dim else 1 for axis in range(len(extent))])
    return gain


def normal_values(stream_key, shape, scale, most, pieces=(), held_as=jnp.bfloat16):
    array = jax.random.normal(stream_key, shape, jnp.float32) * scale
    if len(pieces) > 0:
        array = shard_levels(stream_key, shape, pieces, -0.22, 0.18) * array
    return jnp.clip(array, min=-most, max=most).astype(held_as)


def setup_inputs(seed: int = 0) -> dict:
    key_list = jax.random.split(jax.random.key(seed), 9)
    query = draw_query(jax.random.fold_in(key_list[8], 71), 0)
    fresh_kv = draw_fresh_kv(jax.random.fold_in(key_list[8], 71), 0)
    stale_kv = draw_stale_kv(jax.random.fold_in(key_list[8], 71), 0)
    assign = jax.random.permutation(key_list[3], TOKENS).astype(jnp.int32)
    timestep = jax.random.randint(key_list[4], (1,), 0, STEPS).astype(jnp.int32)
    gate_table = normal_values(key_list[5], (STEPS, D), 1.0, 6.0, ((1, 8),), jnp.float32)
    residual = normal_values(key_list[6], (2, TOKENS, D), 0.3, 1.796875, ((1, 64), (2, 8)))
    out_weight = normal_values(key_list[7], (HEADS * HD, D), (HEADS * HD) ** -0.5, 0.125, ((0, 4), (1, 2)))
    return {"query": query, "fresh_kv": fresh_kv, "stale_kv": stale_kv, "assign": assign, "timestep": timestep, "gate_table": gate_table, "residual": residual, "out_weight": out_weight}


guide_scale = 5.0


def reference(query, fresh_kv, stale_kv, assign, timestep, gate_table, residual, out_weight):
    slab_count = TOKENS // TOK_DEV
    score_scale = HD ** -0.5
    row_ids = jnp.arange(TOKENS, dtype=jnp.int32)

    def attend(item_index):
        branch = item_index // slab_count
        slab = item_index % slab_count
        offset = (slab * TOK_DEV).astype(jnp.int32)
        branch_query = lax.dynamic_index_in_dim(query, branch, 0, keepdims=False)
        branch_fresh = lax.dynamic_index_in_dim(fresh_kv, branch, 0, keepdims=False)
        branch_stale = lax.dynamic_index_in_dim(stale_kv, branch, 0, keepdims=False)
        queries = lax.dynamic_slice_in_dim(branch_query, offset, TOK_DEV, 0)
        fresh_rows = lax.dynamic_slice_in_dim(branch_fresh, offset, TOK_DEV, 1)
        own_rows = lax.dynamic_slice_in_dim(assign, offset, TOK_DEV, 0)
        is_own = jnp.any(row_ids[:, None] == own_rows[None, :], axis=1)
        key_bias = jnp.concatenate([jnp.zeros((TOK_DEV,), jnp.float32), jnp.where(is_own, jnp.float32(-1e30), jnp.float32(0.0))])
        key_rows = jnp.concatenate([fresh_rows[0], branch_stale[0]], axis=0)
        value_rows = jnp.concatenate([fresh_rows[1], branch_stale[1]], axis=0)
        queries = queries.reshape(TOK_DEV, HEADS, HD).astype(jnp.float32)
        key_rows = key_rows.reshape(-1, HEADS, HD).astype(jnp.float32)
        value_rows = value_rows.reshape(-1, HEADS, HD).astype(jnp.float32)
        scores = jnp.einsum('qhd,khd->hqk', queries, key_rows) * score_scale + key_bias[None, None, :]
        maxima = jnp.max(scores, axis=-1, keepdims=True)
        weights = jnp.exp(scores - maxima)
        totals = jnp.sum(weights, axis=-1)
        weights = weights.astype(jnp.bfloat16).astype(jnp.float32)
        attended = jnp.einsum('hqk,khd->hqd', weights, value_rows) / totals[..., None]
        return attended.transpose(1, 0, 2).reshape(TOK_DEV, HEADS * HD).astype(jnp.bfloat16)

    attended = lax.map(attend, jnp.arange(2 * slab_count, dtype=jnp.int32))
    attended = attended.reshape(2, TOKENS, HEADS * HD)
    projected = jnp.stack([jnp.dot(attended[0], out_weight, preferred_element_type=jnp.float32), jnp.dot(attended[1], out_weight, preferred_element_type=jnp.float32)])
    chosen = jnp.arange(STEPS, dtype=jnp.int32) == timestep[0]
    gate_row = jnp.sum(jnp.where(chosen[:, None], gate_table, jnp.float32(0.0)), axis=0)
    block = residual.astype(jnp.float32) + gate_row[None, None, :] * projected
    guided = block[1] + guide_scale * (block[0] - block[1])
    return guided.astype(jnp.bfloat16)
```

```python
import functools

import jax
import jax.numpy as jnp
from jax import lax
from jax.experimental import pallas as pl
from jax.experimental.pallas import tpu as pltpu
from jax.sharding import Mesh
from jax.sharding import PartitionSpec as P

HD = 128
LANES = 128
GUIDE = 5.0
MASKED = -1e30
SCALE = HD**-0.5
VMEM = pl.BlockSpec(memory_space=pltpu.VMEM)
SMEM = pl.BlockSpec(memory_space=pltpu.SMEM)
PARAMS = pltpu.CompilerParams(vmem_limit_bytes=40 * 1024 * 1024)


def shift(value, axis, step):
    size = lax.axis_size(axis)
    return lax.ppermute(value, axis, [(i, (i + step) % size) for i in range(size)])


def head_lanes(head):
    return slice(head * HD, (head + 1) * HD)


def softmax_part(queries, keys, values, bias):
    scores = lax.dot_general(
        queries, keys, (((1,), (1,)), ((), ())), preferred_element_type=jnp.float32
    )
    scores = scores * SCALE
    if bias is not None:
        slabs = bias.shape[0]
        scores = (scores.reshape(slabs, -1, scores.shape[1]) + bias).reshape(scores.shape)
    maxima = jnp.max(scores, axis=1, keepdims=True)
    weights = jnp.exp(scores - maxima)
    totals = jnp.sum(weights, axis=1, keepdims=True)
    update = jnp.dot(weights.astype(jnp.bfloat16), values, preferred_element_type=jnp.float32)
    return update / totals, maxima, totals


def in_three(value):
    high = value.astype(jnp.bfloat16).astype(jnp.float32)
    mid = (value - high).astype(jnp.bfloat16).astype(jnp.float32)
    return [high, mid, value - high - mid]


def fresh_kernel(query_ref, fresh_ref, out_ref, stats_ref):
    rows, width = query_ref.shape
    lane = lax.broadcasted_iota(jnp.int32, (rows, LANES), 1)
    stats = jnp.zeros((rows, LANES), jnp.float32)
    for head in range(width // HD):
        at = head_lanes(head)
        part, maxima, totals = softmax_part(
            query_ref[:, at], fresh_ref[0, :, at], fresh_ref[1, :, at], None
        )
        out_ref[:, at] = part
        stats = jnp.where(lane == 2 * head, maxima, stats)
        stats = jnp.where(lane == 2 * head + 1, totals, stats)
    stats_ref[...] = stats


def stale_kernel(keys_ref, query_ref, *refs):
    blocks, last_key, last_value, out_ref = refs[:-3], refs[-3], refs[-2], refs[-1]
    slabs, rows, wide = query_ref.shape
    width = wide - LANES
    owned = query_ref[:, :, width : width + LANES].astype(jnp.float32)
    key_ids = keys_ref[0:1, :]
    bias = []
    for slab in range(slabs):
        own_ids = owned[slab, :, 0:1] * float(LANES) + owned[slab, :, 1:2]
        bias.append(
            jnp.min(
                jnp.where(own_ids == key_ids, jnp.float32(MASKED), jnp.float32(0.0)),
                axis=0,
                keepdims=True,
            )[None]
        )
    bias = jnp.concatenate(bias, axis=0)
    lane = lax.broadcasted_iota(jnp.int32, (slabs * rows, LANES), 1)
    stats = jnp.zeros((slabs * rows, LANES), jnp.float32)
    for head in range(width // HD):
        at = head_lanes(head)
        keys = jnp.concatenate([b[0, :, at] for b in blocks] + [last_key[:, at]], axis=0)
        values = jnp.concatenate([b[1, :, at] for b in blocks] + [last_value[:, at]], axis=0)
        queries = query_ref[:, :, at].reshape(slabs * rows, HD)
        part, maxima, totals = softmax_part(queries, keys, values, bias)
        out_ref[:, :, at] = part.astype(jnp.bfloat16).reshape(slabs, rows, HD)
        for place, piece in enumerate(in_three(maxima) + in_three(totals)):
            stats = jnp.where(lane == 6 * head + place, piece, stats)
    out_ref[:, :, width:] = stats.astype(jnp.bfloat16).reshape(slabs, rows, LANES)


def combine_kernel(parts_ref, fresh_ref, fresh_stats_ref, out_ref):
    count, rows, wide = parts_ref.shape
    width = wide - LANES
    stats = parts_ref[:, :, width:].astype(jnp.float32)

    def from_three(part, first):
        high, mid, low = (stats[part, :, first + k : first + k + 1] for k in range(3))
        return high + mid + low

    for head in range(width // HD):
        at = head_lanes(head)
        maxima = [from_three(i, 6 * head) for i in range(count)]
        totals = [from_three(i, 6 * head + 3) for i in range(count)]
        maxima.append(fresh_stats_ref[:, 2 * head : 2 * head + 1])
        totals.append(fresh_stats_ref[:, 2 * head + 1 : 2 * head + 2])
        highest = functools.reduce(jnp.maximum, maxima)
        shares = [
            jnp.exp(maximum - highest) * total
            for maximum, total in zip(maxima, totals, strict=True)
        ]
        total = functools.reduce(jnp.add, shares)
        joined = fresh_ref[:, at] * shares[-1]
        for i in range(count):
            joined = joined + parts_ref[i, :, at].astype(jnp.float32) * shares[i]
        out_ref[:, at] = (joined / total).astype(jnp.bfloat16)


def project_kernel(factor_ref, own_ref, other_ref, weight_ref, out_ref):
    mixed = own_ref[...].astype(jnp.float32) * factor_ref[0] + other_ref[...].astype(
        jnp.float32
    ) * factor_ref[1]
    out_ref[0] = jnp.dot(
        mixed.astype(jnp.bfloat16), weight_ref[...], preferred_element_type=jnp.float32
    ).astype(jnp.bfloat16)


def shards(query, fresh_kv, stale_kv, assign, timestep, gate_table, residual, out_weight):
    rows, width = query.shape[1:]
    ring = lax.axis_size("zh")
    slabs = lax.axis_size("x") * lax.axis_size("zl")
    parts = lax.axis_size("t")

    places = jnp.stack([assign // LANES, assign % LANES], axis=1).astype(jnp.bfloat16)
    message = jnp.concatenate(
        [query[0], places, jnp.zeros((rows, LANES - 2), jnp.bfloat16)], axis=1
    )
    queries = lax.all_to_all(
        jnp.broadcast_to(message[None], (slabs, *message.shape)), ("x", "zl"), 0, 0
    )

    own_kv = stale_kv[0]
    blocks, offsets = [own_kv], [0]
    ahead = behind = own_kv
    for step in range(1, ring // 2):
        ahead = shift(ahead, "zh", 1)
        behind = shift(behind, "zh", -1)
        blocks += [ahead, behind]
        offsets += [-step, step]
    last_key = shift(ahead[0], "zh", 1)
    last_value = shift(behind[1], "zh", -1)
    offsets.append(ring // 2)
    z_far = (lax.axis_index("zh") + jnp.array(offsets, jnp.int32)) % ring
    slab_ids = (lax.axis_index("x") * ring + z_far) * lax.axis_size("zl") + lax.axis_index("zl")
    key_ids = (slab_ids[:, None] * rows + jnp.arange(rows, dtype=jnp.int32)).reshape(1, -1)
    key_ids = jnp.broadcast_to(key_ids.astype(jnp.float32), (8, key_ids.shape[1]))

    fresh_out, fresh_stats = pl.pallas_call(
        fresh_kernel,
        out_shape=(
            jax.ShapeDtypeStruct((rows, width), jnp.float32),
            jax.ShapeDtypeStruct((rows, LANES), jnp.float32),
        ),
        in_specs=[VMEM] * 2,
        out_specs=(VMEM, VMEM),
        compiler_params=PARAMS,
        name="fresh",
    )(query[0], fresh_kv[0])

    stale_out = pl.pallas_call(
        stale_kernel,
        out_shape=jax.ShapeDtypeStruct((slabs, rows, width + LANES), jnp.bfloat16),
        in_specs=[VMEM] * (len(blocks) + 4),
        out_specs=VMEM,
        compiler_params=PARAMS,
        name="stale",
    )(key_ids, queries, *blocks, last_key, last_value)
    stale_out = lax.all_to_all(stale_out, ("x", "zl"), 0, 0)

    attended = pl.pallas_call(
        combine_kernel,
        out_shape=jax.ShapeDtypeStruct((rows, width), jnp.bfloat16),
        in_specs=[VMEM] * 3,
        out_specs=VMEM,
        compiler_params=PARAMS,
        name="combine",
    )(stale_out, fresh_out, fresh_stats)

    other = shift(attended, "g", 1)
    factors = jnp.where(
        lax.axis_index("g") == 0,
        jnp.array([GUIDE, 1.0 - GUIDE], jnp.float32),
        jnp.array([1.0 - GUIDE, GUIDE], jnp.float32),
    )
    columns = out_weight.shape[1] // parts
    projected = pl.pallas_call(
        project_kernel,
        out_shape=jax.ShapeDtypeStruct((parts, rows, columns), jnp.bfloat16),
        grid=(parts,),
        in_specs=[
            SMEM,
            pl.BlockSpec((rows, width), lambda i: (0, 0)),
            pl.BlockSpec((rows, width), lambda i: (0, 0)),
            pl.BlockSpec((width, columns), lambda i: (0, i)),
        ],
        out_specs=pl.BlockSpec((1, rows, columns), lambda i: (i, 0, 0)),
        compiler_params=PARAMS,
        name="project",
    )(factors, attended, other, out_weight)
    projected = lax.all_to_all(projected, "t", 0, 0)

    chosen = jnp.arange(gate_table.shape[0], dtype=jnp.int32) == timestep[0]
    gate_row = jnp.sum(jnp.where(chosen[:, None], gate_table, jnp.float32(0.0)), axis=0)
    summed = jnp.sum(projected.astype(jnp.float32), axis=0)
    residual_f = residual.astype(jnp.float32)
    base = residual_f[1] + GUIDE * (residual_f[0] - residual_f[1])
    return (base + gate_row[None, :] * summed).astype(jnp.bfloat16)


def solution(mesh):
    guide, patch, tensor = mesh.devices.shape
    x_size, z_low = 4, 2
    z_high = patch // (x_size * z_low)
    fine = Mesh(
        mesh.devices.reshape(guide, x_size, z_high, z_low, tensor), ("g", "x", "zh", "zl", "t")
    )
    slab = ("x", "zh", "zl")
    placed = (
        P("g", slab, "t"),
        P("g", None, slab, "t"),
        P("g", None, slab, "t"),
        P(slab),
        P(),
        P(None, ("g", "t")),
        P(None, slab, ("g", "t")),
        P("t", "g"),
    )
    return jax.shard_map(
        shards,
        mesh=fine,
        in_specs=placed,
        out_specs=P(slab, ("g", "t")),
        check_vma=False,
    )
```

```python
import functools
import math

import jax
import jax.numpy as jnp
from jax import lax
from jax.experimental import pallas as pl
from jax.experimental.pallas import tpu as pltpu
from jax.sharding import Mesh
from jax.sharding import PartitionSpec as P

HD = 128
LANES = 128
SPAN = 16
GUIDE = 5.0
MASKED = -1e30
EXPONENT = HD**-0.5 * math.log2(math.e)
VMEM = pl.BlockSpec(memory_space=pltpu.VMEM)
SMEM = pl.BlockSpec(memory_space=pltpu.SMEM)
MIB = 1024 * 1024


def shift(value, axis, step):
    size = lax.axis_size(axis)
    return lax.ppermute(value, axis, [(i, (i + step) % size) for i in range(size)])


def head_lanes(head):
    return slice(head * HD, (head + 1) * HD)


def scores_of(queries, keys, bias):
    scores = lax.dot_general(
        queries, keys, (((1,), (1,)), ((), ())), preferred_element_type=jnp.float32
    )
    if bias is not None:
        slabs = bias.shape[0]
        scores = (scores.reshape(slabs, -1, scores.shape[1]) + bias).reshape(scores.shape)
    return scores


def weighted(scores, maxima, values):
    weights = jnp.exp2((scores - maxima) * EXPONENT)
    totals = jnp.sum(weights, axis=1, keepdims=True)
    update = jnp.dot(weights.astype(jnp.bfloat16), values, preferred_element_type=jnp.float32)
    return update, totals


def place_stats(stats, lane, head, maxima, totals):
    stats = jnp.where(lane % SPAN == head, maxima, stats)
    return jnp.where(lane % SPAN == head + SPAN // 2, totals, stats)


def fresh_kernel(query_ref, fresh_ref, out_ref, stats_ref):
    rows, width = query_ref.shape
    lane = lax.broadcasted_iota(jnp.int32, (rows, LANES), 1)
    stats = jnp.zeros((rows, LANES), jnp.float32)
    for head in range(width // HD):
        at = head_lanes(head)
        scores = scores_of(query_ref[:, at], fresh_ref[0, :, at], None)
        maxima = jnp.max(scores, axis=1, keepdims=True)
        update, totals = weighted(scores, maxima, fresh_ref[1, :, at])
        out_ref[:, at] = update / totals
        stats = place_stats(stats, lane, head, maxima, totals)
    stats_ref[...] = stats


def own_bias(query_ref, key_ids):
    slabs, _, wide = query_ref.shape
    owned = query_ref[:, :, wide - LANES :].astype(jnp.float32)
    bias = []
    for slab in range(slabs):
        own_ids = owned[slab, :, 0:1] * float(LANES) + owned[slab, :, 1:2]
        kept = jnp.where(own_ids == key_ids, jnp.float32(MASKED), jnp.float32(0.0))
        bias.append(jnp.min(kept, axis=0, keepdims=True)[None])
    return jnp.concatenate(bias, axis=0)


def stale_kernel(keys_ref, query_ref, *refs):
    blocks, last_key, last_value, out_ref = refs[:-3], refs[-3], refs[-2], refs[-1]
    slabs, rows, wide = query_ref.shape
    bias = own_bias(query_ref, keys_ref[0:1, :])
    lane = lax.broadcasted_iota(jnp.int32, (slabs * rows, LANES), 1)
    stats = jnp.zeros((slabs * rows, LANES), jnp.float32)
    for head in range(wide // HD - 1):
        at = head_lanes(head)
        keys = jnp.concatenate([b[0, :, at] for b in blocks] + [last_key[:, at]], axis=0)
        values = jnp.concatenate([b[1, :, at] for b in blocks] + [last_value[:, at]], axis=0)
        scores = scores_of(query_ref[:, :, at].reshape(slabs * rows, HD), keys, bias)
        maxima = jnp.max(scores, axis=1, keepdims=True)
        update, totals = weighted(scores, maxima, values)
        part = (update / totals).astype(jnp.bfloat16)
        out_ref[:, :, at] = part.reshape(slabs, rows, HD)
        stats = place_stats(stats, lane, head, maxima, totals)
    high = stats.astype(jnp.bfloat16).astype(jnp.float32)
    mid = (stats - high).astype(jnp.bfloat16).astype(jnp.float32)
    low = stats - high - mid
    sent = jnp.where(lane < SPAN, high, jnp.where(lane < 2 * SPAN, mid, low))
    out_ref[:, :, wide - LANES :] = sent.astype(jnp.bfloat16).reshape(slabs, rows, LANES)


def combine_kernel(parts_ref, fresh_ref, fresh_stats_ref, out_ref):
    count, rows, wide = parts_ref.shape
    stats = []
    for part in range(count):
        sent = parts_ref[part, :, wide - LANES :].astype(jnp.float32)
        whole = sent + pltpu.roll(sent, LANES - SPAN, 1) + pltpu.roll(sent, LANES - 2 * SPAN, 1)
        stats.append(whole)
    stats.append(fresh_stats_ref[...])
    highest = functools.reduce(jnp.maximum, stats)
    shares = [
        jnp.exp2((s - highest) * EXPONENT) * pltpu.roll(s, LANES - SPAN // 2, 1) for s in stats
    ]
    total = functools.reduce(jnp.add, shares)
    shares = [share / total for share in shares]
    for head in range(wide // HD - 1):
        at = head_lanes(head)
        joined = fresh_ref[:, at] * shares[-1][:, head : head + 1]
        for part in range(count):
            share = shares[part][:, head : head + 1]
            joined = joined + parts_ref[part, :, at].astype(jnp.float32) * share
        out_ref[:, at] = joined.astype(jnp.bfloat16)


def project_kernel(factor_ref, own_ref, other_ref, weight_ref, out_ref):
    own = own_ref[...].astype(jnp.float32) * factor_ref[0]
    other = other_ref[...].astype(jnp.float32) * factor_ref[1]
    mixed = (own + other).astype(jnp.bfloat16)
    columns = out_ref.shape[2]
    for part in range(out_ref.shape[0]):
        weights = weight_ref[:, part * columns : (part + 1) * columns]
        product = jnp.dot(mixed, weights, preferred_element_type=jnp.float32)
        out_ref[part] = product.astype(jnp.bfloat16)


def local_call(kernel, out_shape, specs, mib):
    return pl.pallas_call(
        kernel,
        out_shape=out_shape,
        in_specs=specs,
        out_specs=jax.tree.map(lambda _: VMEM, out_shape),
        compiler_params=pltpu.CompilerParams(vmem_limit_bytes=mib * MIB),
    )


def shards(query, fresh_kv, stale_kv, assign, timestep, gate_table, residual, out_weight):
    rows, width = query.shape[1:]
    ring = lax.axis_size("zh")
    slabs = lax.axis_size("x") * lax.axis_size("zl")
    parts = lax.axis_size("t")

    places = jnp.stack([assign // LANES, assign % LANES], axis=1).astype(jnp.bfloat16)
    message = jnp.concatenate(
        [query[0], places, jnp.zeros((rows, LANES - 2), jnp.bfloat16)], axis=1
    )

    blocks, offsets = [stale_kv[0]], [0]
    ahead, behind = stale_kv[0], lax.optimization_barrier((stale_kv[0], message))[0]
    for step in range(1, ring // 2):
        ahead = shift(ahead, "zh", 1)
        behind = shift(behind, "zh", -1)
        blocks += [ahead, behind]
        offsets += [-step, step]
    last_key = shift(ahead[0], "zh", 1)
    last_value = shift(behind[1], "zh", -1)
    offsets.append(ring // 2)
    z_far = (lax.axis_index("zh") + jnp.array(offsets, jnp.int32)) % ring
    slab_ids = (lax.axis_index("x") * ring + z_far) * lax.axis_size("zl") + lax.axis_index("zl")
    key_ids = (slab_ids[:, None] * rows + jnp.arange(rows, dtype=jnp.int32)).astype(jnp.float32)
    key_ids = jnp.broadcast_to(key_ids.reshape(1, -1), (8, ring * rows))

    swapped = shift(message, "zl", 1)
    is_low = lax.axis_index("zl") == 0
    pair = jnp.stack(
        [jnp.where(is_low, message, swapped), jnp.where(is_low, swapped, message)]
    )
    queries = lax.all_to_all(
        jnp.broadcast_to(pair[None], (lax.axis_size("x"), *pair.shape)), "x", 0, 0
    ).reshape(slabs, *message.shape)

    sums = jax.ShapeDtypeStruct((rows, width), jnp.float32)
    stats = jax.ShapeDtypeStruct((rows, LANES), jnp.float32)
    fresh_out, fresh_stats = local_call(fresh_kernel, (sums, stats), [VMEM] * 2, 8)(
        query[0], fresh_kv[0]
    )
    parts_out = jax.ShapeDtypeStruct((slabs, rows, width + LANES), jnp.bfloat16)
    parts_out = local_call(stale_kernel, parts_out, [VMEM] * (len(blocks) + 4), 24)(
        key_ids, queries, *blocks, last_key, last_value
    )
    parts_out = lax.all_to_all(parts_out, ("x", "zl"), 0, 0)

    attended = jax.ShapeDtypeStruct((rows, width), jnp.bfloat16)
    attended = local_call(combine_kernel, attended, [VMEM] * 3, 12)(
        parts_out, fresh_out, fresh_stats
    )

    other = shift(attended, "g", 1)
    factors = jnp.where(
        lax.axis_index("g") == 0,
        jnp.array([GUIDE, 1.0 - GUIDE], jnp.float32),
        jnp.array([1.0 - GUIDE, GUIDE], jnp.float32),
    )
    columns = out_weight.shape[1] // parts
    projected = jax.ShapeDtypeStruct((parts, rows, columns), jnp.bfloat16)
    projected = local_call(project_kernel, projected, [SMEM] + [VMEM] * 3, 12)(
        factors, attended, other, out_weight
    )
    projected = lax.all_to_all(projected, "t", 0, 0)

    chosen = jnp.arange(gate_table.shape[0], dtype=jnp.int32) == timestep[0]
    gate_row = jnp.sum(jnp.where(chosen[:, None], gate_table, jnp.float32(0.0)), axis=0)
    summed = jnp.sum(projected.astype(jnp.float32), axis=0)
    residual_f = residual.astype(jnp.float32)
    base = residual_f[1] + GUIDE * (residual_f[0] - residual_f[1])
    return (base + gate_row[None, :] * summed).astype(jnp.bfloat16)


def solution(mesh):
    guide, patch, tensor = mesh.devices.shape
    x_size, z_low = 4, 2
    z_high = patch // (x_size * z_low)
    fine = Mesh(
        mesh.devices.reshape(guide, x_size, z_high, z_low, tensor), ("g", "x", "zh", "zl", "t")
    )
    slab = ("x", "zh", "zl")
    placed = (
        P("g", slab, "t"),
        P("g", None, slab, "t"),
        P("g", None, slab, "t"),
        P(slab),
        P(),
        P(None, ("g", "t")),
        P(None, slab, ("g", "t")),
        P("t", "g"),
    )
    return jax.shard_map(
        shards,
        mesh=fine,
        in_specs=placed,
        out_specs=P(slab, ("g", "t")),
        check_vma=False,
    )
```

```python
import functools
import math

import jax
import jax.numpy as jnp
from jax import lax
from jax.experimental import pallas as pl
from jax.experimental.pallas import tpu as pltpu
from jax.sharding import Mesh
from jax.sharding import PartitionSpec as P

HD = 128
LANES = 128
SPAN = 16
GUIDE = 5.0
MASKED = -1e30
EXPONENT = HD**-0.5 * math.log2(math.e)
VMEM = pl.BlockSpec(memory_space=pltpu.VMEM)
SMEM = pl.BlockSpec(memory_space=pltpu.SMEM)
MIB = 1024 * 1024


def shift(value, axis, step):
    size = lax.axis_size(axis)
    return lax.ppermute(value, axis, [(i, (i + step) % size) for i in range(size)])


def trade(value, step):
    size, parts = lax.axis_size("zh"), lax.axis_size("t")
    pairs = []
    for place in range(size):
        for part in range(parts):
            even = place ^ 1
            odd = (((place - 1) ^ 1) + 1) % size
            partner = even if (step + part) % 2 == 0 else odd
            pairs.append((place * parts + part, partner * parts + part))
    return lax.ppermute(value, ("zh", "t"), pairs)


def head_lanes(head):
    return slice(head * HD, (head + 1) * HD)


def scores_of(queries, keys, bias):
    scores = lax.dot_general(
        queries, keys, (((1,), (1,)), ((), ())), preferred_element_type=jnp.float32
    )
    if bias is not None:
        slabs = bias.shape[0]
        scores = (scores.reshape(slabs, -1, scores.shape[1]) + bias).reshape(scores.shape)
    return scores


def weighted(scores, maxima, values):
    weights = jnp.exp2((scores - maxima) * EXPONENT).astype(jnp.bfloat16)
    beside = jnp.concatenate([values, jnp.ones_like(values)], axis=1)
    both = jnp.dot(weights, beside, preferred_element_type=jnp.float32)
    return both[:, :HD], both[:, HD:]


def place_stats(stats, lane, head, maxima, totals):
    stats = jnp.where(lane % SPAN == head, maxima, stats)
    return jnp.where(lane % SPAN == head + SPAN // 2, totals, stats)


def fresh_kernel(query_ref, fresh_ref, out_ref, stats_ref):
    rows, width = query_ref.shape
    lane = lax.broadcasted_iota(jnp.int32, (rows, LANES), 1)
    stats = jnp.zeros((rows, LANES), jnp.float32)
    for head in range(width // HD):
        at = head_lanes(head)
        scores = scores_of(query_ref[:, at], fresh_ref[0, :, at], None)
        maxima = jnp.max(scores, axis=1, keepdims=True)
        update, totals = weighted(scores, maxima, fresh_ref[1, :, at])
        out_ref[:, at] = update / totals
        stats = place_stats(stats, lane, head, maxima, totals)
    stats_ref[...] = stats


def join_kernel(own_ref, other_ref, out_ref):
    out_ref[0] = own_ref[...]
    out_ref[1] = other_ref[...]


def own_bias(query_ref, key_ids):
    slabs, _, wide = query_ref.shape
    owned = query_ref[:, :, wide - LANES :].astype(jnp.float32)
    bias = []
    for slab in range(slabs):
        own_ids = owned[slab, :, 0:1] * float(LANES) + owned[slab, :, 1:2]
        kept = jnp.where(own_ids == key_ids, jnp.float32(MASKED), jnp.float32(0.0))
        bias.append(jnp.min(kept, axis=0, keepdims=True)[None])
    return jnp.concatenate(bias, axis=0)


def stale_kernel(keys_ref, query_ref, *refs):
    blocks, out_ref = [], refs[-1]
    for ref in refs[:-1]:
        blocks += [ref] if len(ref.shape) == 3 else [ref.at[0], ref.at[1]]
    slabs, rows, wide = query_ref.shape
    bias = own_bias(query_ref, keys_ref[0:1, :])
    lane = lax.broadcasted_iota(jnp.int32, (slabs * rows, LANES), 1)
    stats = jnp.zeros((slabs * rows, LANES), jnp.float32)
    for head in range(wide // HD - 1):
        at = head_lanes(head)
        keys = jnp.concatenate([b[0, :, at] for b in blocks], axis=0)
        values = jnp.concatenate([b[1, :, at] for b in blocks], axis=0)
        scores = scores_of(query_ref[:, :, at].reshape(slabs * rows, HD), keys, bias)
        maxima = jnp.max(scores, axis=1, keepdims=True)
        update, totals = weighted(scores, maxima, values)
        part = (update / totals).astype(jnp.bfloat16)
        out_ref[:, :, at] = part.reshape(slabs, rows, HD)
        stats = place_stats(stats, lane, head, maxima, totals)
    high = stats.astype(jnp.bfloat16).astype(jnp.float32)
    mid = (stats - high).astype(jnp.bfloat16).astype(jnp.float32)
    low = stats - high - mid
    sent = jnp.where(lane < SPAN, high, jnp.where(lane < 2 * SPAN, mid, low))
    out_ref[:, :, wide - LANES :] = sent.astype(jnp.bfloat16).reshape(slabs, rows, LANES)


def combine_kernel(parts_ref, fresh_ref, fresh_stats_ref, out_ref):
    count, rows, wide = parts_ref.shape
    stats = []
    for part in range(count):
        sent = parts_ref[part, :, wide - LANES :].astype(jnp.float32)
        whole = sent + pltpu.roll(sent, LANES - SPAN, 1) + pltpu.roll(sent, LANES - 2 * SPAN, 1)
        stats.append(whole)
    stats.append(fresh_stats_ref[...])
    highest = functools.reduce(jnp.maximum, stats)
    shares = [
        jnp.exp2((s - highest) * EXPONENT) * pltpu.roll(s, LANES - SPAN // 2, 1) for s in stats
    ]
    total = functools.reduce(jnp.add, shares)
    shares = [share / total for share in shares]
    for head in range(wide // HD - 1):
        at = head_lanes(head)
        joined = fresh_ref[:, at] * shares[-1][:, head : head + 1]
        for part in range(count):
            share = shares[part][:, head : head + 1]
            joined = joined + parts_ref[part, :, at].astype(jnp.float32) * share
        out_ref[:, at] = joined.astype(jnp.bfloat16)


def project_kernel(factor_ref, own_ref, other_ref, weight_ref, out_ref):
    own = own_ref[...].astype(jnp.float32) * factor_ref[0]
    other = other_ref[...].astype(jnp.float32) * factor_ref[1]
    mixed = (own + other).astype(jnp.bfloat16)
    columns = out_ref.shape[2]
    for part in range(out_ref.shape[0]):
        weights = weight_ref[:, part * columns : (part + 1) * columns]
        product = jnp.dot(mixed, weights, preferred_element_type=jnp.float32)
        out_ref[part] = product.astype(jnp.bfloat16)


def local_call(kernel, out_shape, specs, mib, flops=0, exps=0):
    return pl.pallas_call(
        kernel,
        out_shape=out_shape,
        in_specs=specs,
        out_specs=jax.tree.map(lambda _: VMEM, out_shape),
        compiler_params=pltpu.CompilerParams(vmem_limit_bytes=mib * MIB),
        cost_estimate=pl.CostEstimate(flops=flops, bytes_accessed=MIB, transcendentals=exps),
    )


def shards(query, fresh_kv, stale_kv, assign, timestep, gate_table, residual, out_weight):
    rows, width = query.shape[1:]
    ring = lax.axis_size("zh")
    slabs = lax.axis_size("x") * lax.axis_size("zl")
    parts = lax.axis_size("t")

    places = jnp.stack([assign // LANES, assign % LANES], axis=1).astype(jnp.bfloat16)
    message = jnp.concatenate(
        [query[0], places, jnp.zeros((rows, LANES - 2), jnp.bfloat16)], axis=1
    )

    own = stale_kv[0]
    first, second = trade(own, 0), trade(own, 1)
    behind = trade(first, 1)
    two = jax.ShapeDtypeStruct((2, *own.shape), own.dtype)
    two = local_call(join_kernel, two, [VMEM] * 2, 4)(second, behind)
    singles, pairs, offsets = [own, first, second, behind], [], [0, 1, -1, -2]
    for step in range(2, ring // 2):
        two = trade(two, step)
        pairs.append(two)
        reach = [2 * (step // 2), 2 * (step // 2) + 1]
        offsets += reach if step % 2 == 0 else [-1 - k for k in reach]
    side = 1 - 2 * ((lax.axis_index("zh") + lax.axis_index("t")) % 2)
    z_far = (lax.axis_index("zh") + side * jnp.array(offsets, jnp.int32)) % ring
    slab_ids = (lax.axis_index("x") * ring + z_far) * lax.axis_size("zl") + lax.axis_index("zl")
    key_ids = (slab_ids[:, None] * rows + jnp.arange(rows, dtype=jnp.int32)).astype(jnp.float32)
    key_ids = jnp.broadcast_to(key_ids.reshape(1, -1), (8, ring * rows))

    swapped = shift(message, "zl", 1)
    is_low = lax.axis_index("zl") == 0
    pair = jnp.stack(
        [jnp.where(is_low, message, swapped), jnp.where(is_low, swapped, message)]
    )
    queries = lax.all_to_all(
        jnp.broadcast_to(pair[None], (lax.axis_size("x"), *pair.shape)), "x", 0, 0
    ).reshape(slabs, *message.shape)

    sums = jax.ShapeDtypeStruct((rows, width), jnp.float32)
    stats = jax.ShapeDtypeStruct((rows, LANES), jnp.float32)
    fresh_out, fresh_stats = local_call(fresh_kernel, (sums, stats), [VMEM] * 2, 4)(
        query[0], fresh_kv[0]
    )
    parts_out = jax.ShapeDtypeStruct((slabs, rows, width + LANES), jnp.bfloat16)
    specs = [VMEM] * (len(singles) + len(pairs) + 2)
    parts_out = local_call(stale_kernel, parts_out, specs, 14, 2**32, 2**22)(
        key_ids, queries, *singles, *pairs
    )
    parts_out = lax.all_to_all(parts_out, ("x", "zl"), 0, 0)

    attended = jax.ShapeDtypeStruct((rows, width), jnp.bfloat16)
    attended = local_call(combine_kernel, attended, [VMEM] * 3, 4)(
        parts_out, fresh_out, fresh_stats
    )

    other = shift(attended, "g", 1)
    factors = jnp.where(
        lax.axis_index("g") == 0,
        jnp.array([GUIDE, 1.0 - GUIDE], jnp.float32),
        jnp.array([1.0 - GUIDE, GUIDE], jnp.float32),
    )
    columns = out_weight.shape[1] // parts
    projected = jax.ShapeDtypeStruct((parts, rows, columns), jnp.bfloat16)
    projected = local_call(project_kernel, projected, [SMEM] + [VMEM] * 3, 6)(
        factors, attended, other, out_weight
    )
    projected = lax.all_to_all(projected, "t", 0, 0)

    chosen = jnp.arange(gate_table.shape[0], dtype=jnp.int32) == timestep[0]
    gate_row = jnp.sum(jnp.where(chosen[:, None], gate_table, jnp.float32(0.0)), axis=0)
    summed = jnp.sum(projected.astype(jnp.float32), axis=0)
    residual_f = residual.astype(jnp.float32)
    base = residual_f[1] + GUIDE * (residual_f[0] - residual_f[1])
    return (base + gate_row[None, :] * summed).astype(jnp.bfloat16)


def solution(mesh):
    guide, patch, tensor = mesh.devices.shape
    x_size, z_low = 4, 2
    z_high = patch // (x_size * z_low)
    fine = Mesh(
        mesh.devices.reshape(guide, x_size, z_high, z_low, tensor), ("g", "x", "zh", "zl", "t")
    )
    slab = ("x", "zh", "zl")
    placed = (
        P("g", slab, "t"),
        P("g", None, slab, "t"),
        P("g", None, slab, "t"),
        P(slab),
        P(),
        P(None, ("g", "t")),
        P(None, slab, ("g", "t")),
        P("t", "g"),
    )
    return jax.shard_map(
        shards,
        mesh=fine,
        in_specs=placed,
        out_specs=P(slab, ("g", "t")),
        check_vma=False,
    )
```

```python
import functools
import math

import jax
import jax.numpy as jnp
from jax import lax
from jax.experimental import pallas as pl
from jax.experimental.pallas import tpu as pltpu
from jax.sharding import Mesh
from jax.sharding import PartitionSpec as P

HD = 128
LANES = 128
SPAN = 16
GUIDE = 5.0
MASKED = -1e30
EXPONENT = HD**-0.5 * math.log2(math.e)
VMEM = pl.BlockSpec(memory_space=pltpu.VMEM)
SMEM = pl.BlockSpec(memory_space=pltpu.SMEM)
MIB = 1024 * 1024


def shift(value, axis, step):
    size = lax.axis_size(axis)
    return lax.ppermute(value, axis, [(i, (i + step) % size) for i in range(size)])


def trade(value, step):
    size, parts = lax.axis_size("zh"), lax.axis_size("t")
    pairs = []
    for place in range(size):
        for part in range(parts):
            even = place ^ 1
            odd = (((place - 1) ^ 1) + 1) % size
            partner = even if (step + part) % 2 == 0 else odd
            pairs.append((place * parts + part, partner * parts + part))
    return lax.ppermute(value, ("zh", "t"), pairs)


def head_lanes(head):
    return slice(head * HD, (head + 1) * HD)


def softmax_sums(queries, keys, values, bias):
    total = keys.shape[0]
    cut = total * 3 // 5 // LANES * LANES
    pieces = [(0, cut), (cut, total)] if cut else [(0, total)]
    scores = []
    for low, high in pieces:
        score = lax.dot_general(
            queries, keys[low:high], (((1,), (1,)), ((), ())), preferred_element_type=jnp.float32
        )
        if bias is not None:
            slabs = bias.shape[0]
            score = score.reshape(slabs, -1, high - low) + bias[:, :, low:high]
            score = score.reshape(-1, high - low)
        scores.append(score)
    maxima = [jnp.max(score, axis=1, keepdims=True) for score in scores]
    maxima = functools.reduce(jnp.maximum, maxima)
    beside = jnp.concatenate([values, jnp.ones_like(values)], axis=1)
    sums = None
    for (low, high), score in zip(pieces, scores, strict=True):
        weights = jnp.exp2((score - maxima) * EXPONENT).astype(jnp.bfloat16)
        part = jnp.dot(weights, beside[low:high], preferred_element_type=jnp.float32)
        sums = part if sums is None else sums + part
    return sums[:, :HD], sums[:, HD:], maxima


def place_stats(stats, lane, head, maxima, totals):
    stats = jnp.where(lane % SPAN == head, maxima, stats)
    return jnp.where(lane % SPAN == head + SPAN // 2, totals, stats)


def fresh_kernel(query_ref, fresh_ref, out_ref, stats_ref):
    rows, width = query_ref.shape
    lane = lax.broadcasted_iota(jnp.int32, (rows, LANES), 1)
    stats = jnp.zeros((rows, LANES), jnp.float32)
    for head in range(width // HD):
        at = head_lanes(head)
        update, totals, maxima = softmax_sums(
            query_ref[:, at], fresh_ref[0, :, at], fresh_ref[1, :, at], None
        )
        out_ref[:, at] = update / totals
        stats = place_stats(stats, lane, head, maxima, totals)
    stats_ref[...] = stats


def join_kernel(own_ref, other_ref, out_ref):
    out_ref[0] = own_ref[...]
    out_ref[1] = other_ref[...]


def own_bias(query_ref, key_ids):
    slabs, _, wide = query_ref.shape
    owned = query_ref[:, :, wide - LANES :].astype(jnp.float32)
    bias = []
    for slab in range(slabs):
        own_ids = owned[slab, :, 0:1] * float(LANES) + owned[slab, :, 1:2]
        kept = jnp.where(own_ids == key_ids, jnp.float32(MASKED), jnp.float32(0.0))
        bias.append(jnp.min(kept, axis=0, keepdims=True)[None])
    return jnp.concatenate(bias, axis=0)


def stale_kernel(keys_ref, query_ref, *refs):
    blocks, out_ref = [], refs[-1]
    for ref in refs[:-1]:
        blocks += [ref] if len(ref.shape) == 3 else [ref.at[0], ref.at[1]]
    slabs, rows, wide = query_ref.shape
    bias = own_bias(query_ref, keys_ref[0:1, :])
    lane = lax.broadcasted_iota(jnp.int32, (slabs * rows, LANES), 1)
    stats = jnp.zeros((slabs * rows, LANES), jnp.float32)
    for head in range(wide // HD - 1):
        at = head_lanes(head)
        keys = jnp.concatenate([b[0, :, at] for b in blocks], axis=0)
        values = jnp.concatenate([b[1, :, at] for b in blocks], axis=0)
        queries = query_ref[:, :, at].reshape(slabs * rows, HD)
        update, totals, maxima = softmax_sums(queries, keys, values, bias)
        part = (update / totals).astype(jnp.bfloat16)
        out_ref[:, :, at] = part.reshape(slabs, rows, HD)
        stats = place_stats(stats, lane, head, maxima, totals)
    high = stats.astype(jnp.bfloat16).astype(jnp.float32)
    mid = (stats - high).astype(jnp.bfloat16).astype(jnp.float32)
    low = stats - high - mid
    sent = jnp.where(lane < SPAN, high, jnp.where(lane < 2 * SPAN, mid, low))
    out_ref[:, :, wide - LANES :] = sent.astype(jnp.bfloat16).reshape(slabs, rows, LANES)


def combine_kernel(parts_ref, fresh_ref, fresh_stats_ref, out_ref):
    count, rows, wide = parts_ref.shape
    stats = []
    for part in range(count):
        sent = parts_ref[part, :, wide - LANES :].astype(jnp.float32)
        whole = sent + pltpu.roll(sent, LANES - SPAN, 1) + pltpu.roll(sent, LANES - 2 * SPAN, 1)
        stats.append(whole)
    stats.append(fresh_stats_ref[...])
    highest = functools.reduce(jnp.maximum, stats)
    shares = [
        jnp.exp2((s - highest) * EXPONENT) * pltpu.roll(s, LANES - SPAN // 2, 1) for s in stats
    ]
    total = functools.reduce(jnp.add, shares)
    shares = [share / total for share in shares]
    for head in range(wide // HD - 1):
        at = head_lanes(head)
        joined = fresh_ref[:, at] * shares[-1][:, head : head + 1]
        for part in range(count):
            share = shares[part][:, head : head + 1]
            joined = joined + parts_ref[part, :, at].astype(jnp.float32) * share
        out_ref[:, at] = joined.astype(jnp.bfloat16)


def project_kernel(factor_ref, own_ref, other_ref, weight_ref, out_ref):
    own = own_ref[...].astype(jnp.float32) * factor_ref[0]
    other = other_ref[...].astype(jnp.float32) * factor_ref[1]
    mixed = (own + other).astype(jnp.bfloat16)
    columns = out_ref.shape[2]
    for part in range(out_ref.shape[0]):
        weights = weight_ref[:, part * columns : (part + 1) * columns]
        product = jnp.dot(mixed, weights, preferred_element_type=jnp.float32)
        out_ref[part] = product.astype(jnp.bfloat16)


def local_call(kernel, out_shape, specs, mib, flops=0, exps=0):
    return pl.pallas_call(
        kernel,
        out_shape=out_shape,
        in_specs=specs,
        out_specs=jax.tree.map(lambda _: VMEM, out_shape),
        compiler_params=pltpu.CompilerParams(vmem_limit_bytes=mib * MIB),
        cost_estimate=pl.CostEstimate(flops=flops, bytes_accessed=MIB, transcendentals=exps),
    )


def shards(query, fresh_kv, stale_kv, assign, timestep, gate_table, residual, out_weight):
    rows, width = query.shape[1:]
    ring = lax.axis_size("zh")
    slabs = lax.axis_size("x") * lax.axis_size("zl")
    parts = lax.axis_size("t")

    places = jnp.stack([assign // LANES, assign % LANES], axis=1).astype(jnp.bfloat16)
    message = jnp.concatenate(
        [query[0], places, jnp.zeros((rows, LANES - 2), jnp.bfloat16)], axis=1
    )

    own = stale_kv[0]
    first, second = trade(own, 0), trade(own, 1)
    behind = trade(first, 1)
    two = jax.ShapeDtypeStruct((2, *own.shape), own.dtype)
    two = local_call(join_kernel, two, [VMEM] * 2, 4)(second, behind)
    singles, pairs, offsets = [own, first, second, behind], [], [0, 1, -1, -2]
    for step in range(2, ring // 2):
        two = trade(two, step)
        pairs.append(two)
        reach = [2 * (step // 2), 2 * (step // 2) + 1]
        offsets += reach if step % 2 == 0 else [-1 - k for k in reach]
    side = 1 - 2 * ((lax.axis_index("zh") + lax.axis_index("t")) % 2)
    z_far = (lax.axis_index("zh") + side * jnp.array(offsets, jnp.int32)) % ring
    slab_ids = (lax.axis_index("x") * ring + z_far) * lax.axis_size("zl") + lax.axis_index("zl")
    key_ids = (slab_ids[:, None] * rows + jnp.arange(rows, dtype=jnp.int32)).astype(jnp.float32)
    key_ids = jnp.broadcast_to(key_ids.reshape(1, -1), (8, ring * rows))

    swapped = shift(message, "zl", 1)
    is_low = lax.axis_index("zl") == 0
    pair = jnp.stack(
        [jnp.where(is_low, message, swapped), jnp.where(is_low, swapped, message)]
    )
    queries = lax.all_to_all(
        jnp.broadcast_to(pair[None], (lax.axis_size("x"), *pair.shape)), "x", 0, 0
    ).reshape(slabs, *message.shape)

    sums = jax.ShapeDtypeStruct((rows, width), jnp.float32)
    stats = jax.ShapeDtypeStruct((rows, LANES), jnp.float32)
    fresh_out, fresh_stats = local_call(fresh_kernel, (sums, stats), [VMEM] * 2, 4, 2**33, 2**20)(
        query[0], fresh_kv[0]
    )
    parts_out = jax.ShapeDtypeStruct((slabs, rows, width + LANES), jnp.bfloat16)
    specs = [VMEM] * (len(singles) + len(pairs) + 2)
    parts_out = local_call(stale_kernel, parts_out, specs, 14, 2**33, 2**22)(
        key_ids, queries, *singles, *pairs
    )
    parts_out = lax.all_to_all(parts_out, ("x", "zl"), 0, 0)

    attended = jax.ShapeDtypeStruct((rows, width), jnp.bfloat16)
    attended = local_call(combine_kernel, attended, [VMEM] * 3, 4, 2**33, 2**20)(
        parts_out, fresh_out, fresh_stats
    )

    other = shift(attended, "g", 1)
    factors = jnp.where(
        lax.axis_index("g") == 0,
        jnp.array([GUIDE, 1.0 - GUIDE], jnp.float32),
        jnp.array([1.0 - GUIDE, GUIDE], jnp.float32),
    )
    columns = out_weight.shape[1] // parts
    projected = jax.ShapeDtypeStruct((parts, rows, columns), jnp.bfloat16)
    projected = local_call(project_kernel, projected, [SMEM] + [VMEM] * 3, 6)(
        factors, attended, other, out_weight
    )
    projected = lax.all_to_all(projected, "t", 0, 0)

    chosen = jnp.arange(gate_table.shape[0], dtype=jnp.int32) == timestep[0]
    gate_row = jnp.sum(jnp.where(chosen[:, None], gate_table, jnp.float32(0.0)), axis=0)
    summed = jnp.sum(projected.astype(jnp.float32), axis=0)
    residual_f = residual.astype(jnp.float32)
    base = residual_f[1] + GUIDE * (residual_f[0] - residual_f[1])
    return (base + gate_row[None, :] * summed).astype(jnp.bfloat16)


def solution(mesh):
    guide, patch, tensor = mesh.devices.shape
    x_size, z_low = 4, 2
    z_high = patch // (x_size * z_low)
    fine = Mesh(
        mesh.devices.reshape(guide, x_size, z_high, z_low, tensor), ("g", "x", "zh", "zl", "t")
    )
    slab = ("x", "zh", "zl")
    placed = (
        P("g", slab, "t"),
        P("g", None, slab, "t"),
        P("g", None, slab, "t"),
        P(slab),
        P(),
        P(None, ("g", "t")),
        P(None, slab, ("g", "t")),
        P("t", "g"),
    )
    return jax.shard_map(
        shards,
        mesh=fine,
        in_specs=placed,
        out_specs=P(slab, ("g", "t")),
        check_vma=False,
    )
```

```python
import functools
import math

import jax
import jax.numpy as jnp
from jax import lax
from jax.experimental import pallas as pl
from jax.experimental.pallas import tpu as pltpu
from jax.sharding import Mesh
from jax.sharding import PartitionSpec as P

HD = 128
LANES = 128
SPAN = 16
GUIDE = 5.0
MASKED = -1e30
EXPONENT = HD**-0.5 * math.log2(math.e)
VMEM = pl.BlockSpec(memory_space=pltpu.VMEM)
SMEM = pl.BlockSpec(memory_space=pltpu.SMEM)
MIB = 1024 * 1024


def shift(value, axis, step):
    size = lax.axis_size(axis)
    return lax.ppermute(value, axis, [(i, (i + step) % size) for i in range(size)])


def trade(value, step):
    size, parts = lax.axis_size("zh"), lax.axis_size("t")
    pairs = []
    for place in range(size):
        for part in range(parts):
            even = place ^ 1
            odd = (((place - 1) ^ 1) + 1) % size
            partner = even if (step + part) % 2 == 0 else odd
            pairs.append((place * parts + part, partner * parts + part))
    return lax.ppermute(value, ("zh", "t"), pairs)


def head_lanes(head):
    return slice(head * HD, (head + 1) * HD)


def pieces_of(total):
    cut = total * 3 // 5 // LANES * LANES
    return [(0, cut), (cut, total)] if cut else [(0, total)]


def scores_of(queries, keys, bias):
    scores = []
    for low, high in pieces_of(keys.shape[0]):
        score = lax.dot_general(
            queries, keys[low:high], (((1,), (1,)), ((), ())), preferred_element_type=jnp.float32
        )
        if bias is not None:
            slabs = bias.shape[0]
            score = score.reshape(slabs, -1, high - low) + bias[:, :, low:high]
            score = score.reshape(-1, high - low)
        scores.append(score)
    return scores


def softmax_sums(scores, values):
    maxima = [jnp.max(score, axis=1, keepdims=True) for score in scores]
    maxima = functools.reduce(jnp.maximum, maxima)
    weights = [jnp.exp2((score - maxima) * EXPONENT).astype(jnp.bfloat16) for score in scores]
    beside = jnp.concatenate([values, jnp.ones_like(values)], axis=1)
    sums = None
    for (low, high), weight in zip(pieces_of(values.shape[0]), weights, strict=True):
        part = jnp.dot(weight, beside[low:high], preferred_element_type=jnp.float32)
        sums = part if sums is None else sums + part
    return sums[:, :HD], sums[:, HD:], maxima


def place_stats(stats, lane, head, maxima, totals):
    stats = jnp.where(lane % SPAN == head, maxima, stats)
    return jnp.where(lane % SPAN == head + SPAN // 2, totals, stats)


def fresh_kernel(query_ref, fresh_ref, out_ref, stats_ref):
    rows, width = query_ref.shape
    lane = lax.broadcasted_iota(jnp.int32, (rows, LANES), 1)
    stats = jnp.zeros((rows, LANES), jnp.float32)
    for head in range(width // HD):
        at = head_lanes(head)
        scores = scores_of(query_ref[:, at], fresh_ref[0, :, at], None)
        update, totals, maxima = softmax_sums(scores, fresh_ref[1, :, at])
        out_ref[:, at] = update / totals
        stats = place_stats(stats, lane, head, maxima, totals)
    stats_ref[...] = stats


def join_kernel(own_ref, other_ref, out_ref):
    out_ref[0] = own_ref[...]
    out_ref[1] = other_ref[...]


def own_bias(query_ref, key_ids):
    slabs, _, wide = query_ref.shape
    owned = query_ref[:, :, wide - LANES :].astype(jnp.float32)
    bias = []
    for slab in range(slabs):
        own_ids = owned[slab, :, 0:1] * float(LANES) + owned[slab, :, 1:2]
        kept = jnp.where(own_ids == key_ids, jnp.float32(MASKED), jnp.float32(0.0))
        bias.append(jnp.min(kept, axis=0, keepdims=True)[None])
    return jnp.concatenate(bias, axis=0)


def stale_kernel(keys_ref, query_ref, *refs):
    blocks, out_ref = [], refs[-1]
    for ref in refs[:-1]:
        blocks += [ref] if len(ref.shape) == 3 else [ref.at[0], ref.at[1]]
    slabs, rows, wide = query_ref.shape
    bias = own_bias(query_ref, keys_ref[0:1, :])
    lane = lax.broadcasted_iota(jnp.int32, (slabs * rows, LANES), 1)
    stats = jnp.zeros((slabs * rows, LANES), jnp.float32)
    heads = wide // HD - 1

    def head_scores(head):
        at = head_lanes(head)
        keys = jnp.concatenate([b[0, :, at] for b in blocks], axis=0)
        return scores_of(query_ref[:, :, at].reshape(slabs * rows, HD), keys, bias)

    scores = head_scores(0)
    for head in range(heads):
        at = head_lanes(head)
        later = head_scores(head + 1) if head + 1 < heads else None
        values = jnp.concatenate([b[1, :, at] for b in blocks], axis=0)
        update, totals, maxima = softmax_sums(scores, values)
        part = (update / totals).astype(jnp.bfloat16).reshape(slabs, rows, HD)
        for slab in range(slabs):
            out_ref[slab % 2 * (slabs // 2) + slab // 2, :, at] = part[slab]
        stats = place_stats(stats, lane, head, maxima, totals)
        scores = later
    high = stats.astype(jnp.bfloat16).astype(jnp.float32)
    mid = (stats - high).astype(jnp.bfloat16).astype(jnp.float32)
    low = stats - high - mid
    sent = jnp.where(lane < SPAN, high, jnp.where(lane < 2 * SPAN, mid, low))
    sent = sent.astype(jnp.bfloat16).reshape(slabs, rows, LANES)
    for slab in range(slabs):
        out_ref[slab % 2 * (slabs // 2) + slab // 2, :, wide - LANES :] = sent[slab]


def combine_kernel(parts_ref, fresh_ref, fresh_stats_ref, out_ref):
    count, rows, wide = parts_ref.shape
    stats = []
    for part in range(count):
        sent = parts_ref[part, :, wide - LANES :].astype(jnp.float32)
        whole = sent + pltpu.roll(sent, LANES - SPAN, 1) + pltpu.roll(sent, LANES - 2 * SPAN, 1)
        stats.append(whole)
    stats.append(fresh_stats_ref[...])
    highest = functools.reduce(jnp.maximum, stats)
    shares = [
        jnp.exp2((s - highest) * EXPONENT) * pltpu.roll(s, LANES - SPAN // 2, 1) for s in stats
    ]
    total = functools.reduce(jnp.add, shares)
    shares = [share / total for share in shares]
    for head in range(wide // HD - 1):
        at = head_lanes(head)
        joined = fresh_ref[:, at] * shares[-1][:, head : head + 1]
        for part in range(count):
            share = shares[part][:, head : head + 1]
            joined = joined + parts_ref[part, :, at].astype(jnp.float32) * share
        out_ref[:, at] = joined.astype(jnp.bfloat16)


def project_kernel(factor_ref, own_ref, other_ref, weight_ref, out_ref):
    own = own_ref[...].astype(jnp.float32) * factor_ref[0]
    other = other_ref[...].astype(jnp.float32) * factor_ref[1]
    mixed = (own + other).astype(jnp.bfloat16)
    columns = out_ref.shape[2]
    for part in range(out_ref.shape[0]):
        weights = weight_ref[:, part * columns : (part + 1) * columns]
        product = jnp.dot(mixed, weights, preferred_element_type=jnp.float32)
        out_ref[part] = product.astype(jnp.bfloat16)


def local_call(kernel, out_shape, specs, mib, flops=0, exps=0):
    return pl.pallas_call(
        kernel,
        out_shape=out_shape,
        in_specs=specs,
        out_specs=jax.tree.map(lambda _: VMEM, out_shape),
        compiler_params=pltpu.CompilerParams(vmem_limit_bytes=mib * MIB),
        cost_estimate=pl.CostEstimate(flops=flops, bytes_accessed=MIB, transcendentals=exps),
    )


def shards(query, fresh_kv, stale_kv, assign, timestep, gate_table, residual, out_weight):
    rows, width = query.shape[1:]
    ring = lax.axis_size("zh")
    slabs = lax.axis_size("x") * lax.axis_size("zl")
    parts = lax.axis_size("t")

    places = jnp.stack([assign // LANES, assign % LANES], axis=1).astype(jnp.bfloat16)
    message = jnp.concatenate(
        [query[0], places, jnp.zeros((rows, LANES - 2), jnp.bfloat16)], axis=1
    )

    own = stale_kv[0]
    first, second = trade(own, 0), trade(own, 1)
    behind = trade(first, 1)
    two = jax.ShapeDtypeStruct((2, *own.shape), own.dtype)
    two = local_call(join_kernel, two, [VMEM] * 2, 4)(second, behind)
    singles, pairs, offsets = [own, first, second, behind], [], [0, 1, -1, -2]
    for step in range(2, ring // 2):
        two = trade(two, step)
        pairs.append(two)
        reach = [2 * (step // 2), 2 * (step // 2) + 1]
        offsets += reach if step % 2 == 0 else [-1 - k for k in reach]
    side = 1 - 2 * ((lax.axis_index("zh") + lax.axis_index("t")) % 2)
    z_far = (lax.axis_index("zh") + side * jnp.array(offsets, jnp.int32)) % ring
    slab_ids = (lax.axis_index("x") * ring + z_far) * lax.axis_size("zl") + lax.axis_index("zl")
    key_ids = (slab_ids[:, None] * rows + jnp.arange(rows, dtype=jnp.int32)).astype(jnp.float32)
    key_ids = jnp.broadcast_to(key_ids.reshape(1, -1), (8, ring * rows))

    swapped = shift(message, "zl", 1)
    is_low = lax.axis_index("zl") == 0
    pair = jnp.stack(
        [jnp.where(is_low, message, swapped), jnp.where(is_low, swapped, message)]
    )
    queries = lax.all_to_all(
        jnp.broadcast_to(pair[None], (lax.axis_size("x"), *pair.shape)), "x", 0, 0
    ).reshape(slabs, *message.shape)

    sums = jax.ShapeDtypeStruct((rows, width), jnp.float32)
    stats = jax.ShapeDtypeStruct((rows, LANES), jnp.float32)
    fresh_out, fresh_stats = local_call(fresh_kernel, (sums, stats), [VMEM] * 2, 4, 2**33, 2**20)(
        query[0], fresh_kv[0]
    )
    parts_out = jax.ShapeDtypeStruct((slabs, rows, width + LANES), jnp.bfloat16)
    specs = [VMEM] * (len(singles) + len(pairs) + 2)
    parts_out = local_call(stale_kernel, parts_out, specs, 14, 2**33, 2**22)(
        key_ids, queries, *singles, *pairs
    )
    parts_out = lax.all_to_all(parts_out, ("zl", "x"), 0, 0)

    attended = jax.ShapeDtypeStruct((rows, width), jnp.bfloat16)
    attended = local_call(combine_kernel, attended, [VMEM] * 3, 4, 2**33, 2**20)(
        parts_out, fresh_out, fresh_stats
    )

    other = shift(attended, "g", 1)
    factors = jnp.where(
        lax.axis_index("g") == 0,
        jnp.array([GUIDE, 1.0 - GUIDE], jnp.float32),
        jnp.array([1.0 - GUIDE, GUIDE], jnp.float32),
    )
    columns = out_weight.shape[1] // parts
    projected = jax.ShapeDtypeStruct((parts, rows, columns), jnp.bfloat16)
    projected = local_call(project_kernel, projected, [SMEM] + [VMEM] * 3, 6)(
        factors, attended, other, out_weight
    )
    projected = lax.all_to_all(projected, "t", 0, 0)

    chosen = jnp.arange(gate_table.shape[0], dtype=jnp.int32) == timestep[0]
    gate_row = jnp.sum(jnp.where(chosen[:, None], gate_table, jnp.float32(0.0)), axis=0)
    summed = jnp.sum(projected.astype(jnp.float32), axis=0)
    residual_f = residual.astype(jnp.float32)
    base = residual_f[1] + GUIDE * (residual_f[0] - residual_f[1])
    return (base + gate_row[None, :] * summed).astype(jnp.bfloat16)


def solution(mesh):
    guide, patch, tensor = mesh.devices.shape
    x_size, z_low = 4, 2
    z_high = patch // (x_size * z_low)
    fine = Mesh(
        mesh.devices.reshape(guide, x_size, z_high, z_low, tensor), ("g", "x", "zh", "zl", "t")
    )
    slab = ("x", "zh", "zl")
    placed = (
        P("g", slab, "t"),
        P("g", None, slab, "t"),
        P("g", None, slab, "t"),
        P(slab),
        P(),
        P(None, ("g", "t")),
        P(None, slab, ("g", "t")),
        P("t", "g"),
    )
    return jax.shard_map(
        shards,
        mesh=fine,
        in_specs=placed,
        out_specs=P(slab, ("g", "t")),
        check_vma=False,
    )
```

```python
import functools
import math

import jax
import jax.numpy as jnp
from jax import lax
from jax.experimental import pallas as pl
from jax.experimental.pallas import tpu as pltpu
from jax.sharding import Mesh
from jax.sharding import PartitionSpec as P

HD = 128
LANES = 128
SPAN = 16
GUIDE = 5.0
MASKED = -1e30
EXPONENT = HD**-0.5 * math.log2(math.e)
VMEM = pl.BlockSpec(memory_space=pltpu.VMEM)
SMEM = pl.BlockSpec(memory_space=pltpu.SMEM)
MIB = 1024 * 1024


def shift(value, axis, step):
    size = lax.axis_size(axis)
    return lax.ppermute(value, axis, [(i, (i + step) % size) for i in range(size)])


def trade(value, step):
    size, parts = lax.axis_size("zh"), lax.axis_size("t")
    pairs = []
    for place in range(size):
        for part in range(parts):
            even = place ^ 1
            odd = (((place - 1) ^ 1) + 1) % size
            partner = even if (step + part) % 2 == 0 else odd
            pairs.append((place * parts + part, partner * parts + part))
    return lax.ppermute(value, ("zh", "t"), pairs)


def head_lanes(head):
    return slice(head * HD, (head + 1) * HD)


def pieces_of(total):
    cut = total * 3 // 5 // LANES * LANES
    return [(0, cut), (cut, total)] if cut else [(0, total)]


def scores_of(queries, keys, bias):
    scores = []
    for low, high in pieces_of(keys.shape[0]):
        score = lax.dot_general(
            queries, keys[low:high], (((1,), (1,)), ((), ())), preferred_element_type=jnp.float32
        )
        if bias is not None:
            slabs = bias.shape[0]
            score = score.reshape(slabs, -1, high - low) + bias[:, :, low:high]
            score = score.reshape(-1, high - low)
        scores.append(score)
    return scores


def softmax_sums(scores, values):
    maxima = [jnp.max(score, axis=1, keepdims=True) for score in scores]
    maxima = functools.reduce(jnp.maximum, maxima)
    weights = [jnp.exp2((score - maxima) * EXPONENT).astype(jnp.bfloat16) for score in scores]
    beside = jnp.concatenate([values, jnp.ones_like(values)], axis=1)
    sums = None
    for (low, high), weight in zip(pieces_of(values.shape[0]), weights, strict=True):
        part = jnp.dot(weight, beside[low:high], preferred_element_type=jnp.float32)
        sums = part if sums is None else sums + part
    return sums[:, :HD], sums[:, HD:], maxima


def place_stats(stats, lane, head, maxima, totals):
    stats = jnp.where(lane % SPAN == head, maxima, stats)
    return jnp.where(lane % SPAN == head + SPAN // 2, totals, stats)


def fresh_kernel(query_ref, fresh_ref, out_ref, stats_ref):
    rows, width = query_ref.shape
    lane = lax.broadcasted_iota(jnp.int32, (rows, LANES), 1)
    stats = jnp.zeros((rows, LANES), jnp.float32)
    for head in range(width // HD):
        at = head_lanes(head)
        scores = scores_of(query_ref[:, at], fresh_ref[0, :, at], None)
        update, totals, maxima = softmax_sums(scores, fresh_ref[1, :, at])
        out_ref[:, at] = update / totals
        stats = place_stats(stats, lane, head, maxima, totals)
    stats_ref[...] = stats


def join_kernel(own_ref, other_ref, out_ref):
    out_ref[0] = own_ref[...]
    out_ref[1] = other_ref[...]


def own_bias(query_ref, key_ids):
    slabs, _, wide = query_ref.shape
    owned = query_ref[:, :, wide - LANES :].astype(jnp.float32)
    bias = []
    for slab in range(slabs):
        own_ids = owned[slab, :, 0:1] * float(LANES) + owned[slab, :, 1:2]
        kept = jnp.where(own_ids == key_ids, jnp.float32(MASKED), jnp.float32(0.0))
        bias.append(jnp.min(kept, axis=0, keepdims=True)[None])
    return jnp.concatenate(bias, axis=0)


def stale_kernel(keys_ref, query_ref, *refs):
    blocks, out_ref = [], refs[-1]
    for ref in refs[:-1]:
        blocks += [ref] if len(ref.shape) == 3 else [ref.at[0], ref.at[1]]
    slabs, rows, wide = query_ref.shape
    bias = own_bias(query_ref, keys_ref[0:1, :])
    lane = lax.broadcasted_iota(jnp.int32, (slabs * rows, LANES), 1)
    stats = jnp.zeros((slabs * rows, LANES), jnp.float32)
    heads = wide // HD - 1

    def head_scores(head):
        at = head_lanes(head)
        keys = jnp.concatenate([b[0, :, at] for b in blocks], axis=0)
        return scores_of(query_ref[:, :, at].reshape(slabs * rows, HD), keys, bias)

    scores = head_scores(0)
    for head in range(heads):
        at = head_lanes(head)
        later = head_scores(head + 1) if head + 1 < heads else None
        values = jnp.concatenate([b[1, :, at] for b in blocks], axis=0)
        update, totals, maxima = softmax_sums(scores, values)
        part = (update / totals).astype(jnp.bfloat16).reshape(slabs, rows, HD)
        for slab in range(slabs):
            out_ref[slab % 2 * (slabs // 2) + slab // 2, :, at] = part[slab]
        stats = place_stats(stats, lane, head, maxima, totals)
        scores = later
    high = stats.astype(jnp.bfloat16).astype(jnp.float32)
    mid = (stats - high).astype(jnp.bfloat16).astype(jnp.float32)
    low = stats - high - mid
    sent = jnp.where(lane < SPAN, high, jnp.where(lane < 2 * SPAN, mid, low))
    sent = sent.astype(jnp.bfloat16).reshape(slabs, rows, LANES)
    for slab in range(slabs):
        out_ref[slab % 2 * (slabs // 2) + slab // 2, :, wide - LANES :] = sent[slab]


def combine_kernel(parts_ref, fresh_ref, fresh_stats_ref, out_ref):
    count, rows, wide = parts_ref.shape
    stats = []
    for part in range(count):
        sent = parts_ref[part, :, wide - LANES :].astype(jnp.float32)
        whole = sent + pltpu.roll(sent, LANES - SPAN, 1) + pltpu.roll(sent, LANES - 2 * SPAN, 1)
        stats.append(whole)
    stats.append(fresh_stats_ref[...])
    highest = functools.reduce(jnp.maximum, stats)
    shares = [
        jnp.exp2((s - highest) * EXPONENT) * pltpu.roll(s, LANES - SPAN // 2, 1) for s in stats
    ]
    total = functools.reduce(jnp.add, shares)
    shares = [share / total for share in shares]
    for head in range(wide // HD - 1):
        at = head_lanes(head)
        joined = fresh_ref[:, at] * shares[-1][:, head : head + 1]
        for part in range(count):
            share = shares[part][:, head : head + 1]
            joined = joined + parts_ref[part, :, at].astype(jnp.float32) * share
        out_ref[:, at] = joined.astype(jnp.bfloat16)


def project_kernel(factor_ref, own_ref, other_ref, weight_ref, out_ref):
    own = own_ref[...].astype(jnp.float32) * factor_ref[0]
    other = other_ref[...].astype(jnp.float32) * factor_ref[1]
    mixed = (own + other).astype(jnp.bfloat16)
    columns = out_ref.shape[2]
    for part in range(out_ref.shape[0]):
        weights = weight_ref[:, part * columns : (part + 1) * columns]
        product = jnp.dot(mixed, weights, preferred_element_type=jnp.float32)
        out_ref[part] = product.astype(jnp.bfloat16)


def local_call(kernel, out_shape, specs, mib, flops=0, exps=0):
    return pl.pallas_call(
        kernel,
        out_shape=out_shape,
        in_specs=specs,
        out_specs=jax.tree.map(lambda _: VMEM, out_shape),
        compiler_params=pltpu.CompilerParams(vmem_limit_bytes=mib * MIB),
        cost_estimate=pl.CostEstimate(flops=flops, bytes_accessed=MIB, transcendentals=exps),
    )


def shards(query, fresh_kv, stale_kv, assign, timestep, gate_table, residual, out_weight):
    rows, width = query.shape[1:]
    ring = lax.axis_size("zh")
    slabs = lax.axis_size("x") * lax.axis_size("zl")
    parts = lax.axis_size("t")

    own = stale_kv[0]
    first, second = trade(own, 0), trade(own, 1)
    behind = trade(first, 1)
    two = jax.ShapeDtypeStruct((2, *own.shape), own.dtype)
    two = local_call(join_kernel, two, [VMEM] * 2, 4)(second, behind)
    singles, pairs, offsets = [own, first, second, behind], [], [0, 1, -1, -2]
    for step in range(2, ring // 2):
        two = trade(two, step)
        pairs.append(two)
        reach = [2 * (step // 2), 2 * (step // 2) + 1]
        offsets += reach if step % 2 == 0 else [-1 - k for k in reach]
    side = 1 - 2 * ((lax.axis_index("zh") + lax.axis_index("t")) % 2)
    z_far = (lax.axis_index("zh") + side * jnp.array(offsets, jnp.int32)) % ring
    slab_ids = (lax.axis_index("x") * ring + z_far) * lax.axis_size("zl") + lax.axis_index("zl")
    key_ids = (slab_ids[:, None] * rows + jnp.arange(rows, dtype=jnp.int32)).astype(jnp.float32)
    key_ids = jnp.broadcast_to(key_ids.reshape(1, -1), (8, ring * rows))

    assign, _ = lax.optimization_barrier((assign, second))
    places = jnp.stack([assign // LANES, assign % LANES], axis=1).astype(jnp.bfloat16)
    message = jnp.concatenate(
        [query[0], places, jnp.zeros((rows, LANES - 2), jnp.bfloat16)], axis=1
    )
    swapped = shift(message, "zl", 1)
    is_low = lax.axis_index("zl") == 0
    pair = jnp.stack(
        [jnp.where(is_low, message, swapped), jnp.where(is_low, swapped, message)]
    )
    queries = lax.all_to_all(
        jnp.broadcast_to(pair[None], (lax.axis_size("x"), *pair.shape)), "x", 0, 0
    ).reshape(slabs, *message.shape)

    sums = jax.ShapeDtypeStruct((rows, width), jnp.float32)
    stats = jax.ShapeDtypeStruct((rows, LANES), jnp.float32)
    fresh_out, fresh_stats = local_call(fresh_kernel, (sums, stats), [VMEM] * 2, 4, 2**33, 2**20)(
        query[0], fresh_kv[0]
    )
    parts_out = jax.ShapeDtypeStruct((slabs, rows, width + LANES), jnp.bfloat16)
    specs = [VMEM] * (len(singles) + len(pairs) + 2)
    parts_out = local_call(stale_kernel, parts_out, specs, 14, 2**33, 2**22)(
        key_ids, queries, *singles, *pairs
    )
    parts_out = lax.all_to_all(parts_out, ("zl", "x"), 0, 0)

    attended = jax.ShapeDtypeStruct((rows, width), jnp.bfloat16)
    attended = local_call(combine_kernel, attended, [VMEM] * 3, 4, 2**33, 2**20)(
        parts_out, fresh_out, fresh_stats
    )

    other = shift(attended, "g", 1)
    factors = jnp.where(
        lax.axis_index("g") == 0,
        jnp.array([GUIDE, 1.0 - GUIDE], jnp.float32),
        jnp.array([1.0 - GUIDE, GUIDE], jnp.float32),
    )
    columns = out_weight.shape[1] // parts
    projected = jax.ShapeDtypeStruct((parts, rows, columns), jnp.bfloat16)
    projected = local_call(project_kernel, projected, [SMEM] + [VMEM] * 3, 6)(
        factors, attended, other, out_weight
    )
    projected = lax.all_to_all(projected, "t", 0, 0)

    chosen = jnp.arange(gate_table.shape[0], dtype=jnp.int32) == timestep[0]
    gate_row = jnp.sum(jnp.where(chosen[:, None], gate_table, jnp.float32(0.0)), axis=0)
    summed = jnp.sum(projected.astype(jnp.float32), axis=0)
    residual_f = residual.astype(jnp.float32)
    base = residual_f[1] + GUIDE * (residual_f[0] - residual_f[1])
    return (base + gate_row[None, :] * summed).astype(jnp.bfloat16)


def solution(mesh):
    guide, patch, tensor = mesh.devices.shape
    x_size, z_low = 4, 2
    z_high = patch // (x_size * z_low)
    fine = Mesh(
        mesh.devices.reshape(guide, x_size, z_high, z_low, tensor), ("g", "x", "zh", "zl", "t")
    )
    slab = ("x", "zh", "zl")
    placed = (
        P("g", slab, "t"),
        P("g", None, slab, "t"),
        P("g", None, slab, "t"),
        P(slab),
        P(),
        P(None, ("g", "t")),
        P(None, slab, ("g", "t")),
        P("t", "g"),
    )
    return jax.shard_map(
        shards,
        mesh=fine,
        in_specs=placed,
        out_specs=P(slab, ("g", "t")),
        check_vma=False,
    )
```
